32 devices in a mesh: grp: 2 (over core), blk: 16 (over z, y, x).
Axes of the slice: x: 2, y: 2, z: 4, core: 2. Of those that a mesh axis runs over, the one named last changes fastest.
Arguments:
- factors: bfloat16 [128, 256, 512], P(('grp', 'blk')), may hold values from -6 to 6
- loadings: bfloat16 [512, 2048], replicated, may hold values from -0.25 to 0.25
- netload_map: bfloat16 [512, 200], replicated, may hold values from -0.25 to 0.25
- rule_weights: bfloat16 [16, 2048, 200], P('blk'), may hold values from -0.125 to 0.125
- rule_bias: float32 [16, 200], P('blk'), may hold values from -3 to 3
Outputs:
- decisions: bfloat16 [256, 128, 200], P('blk', 'grp')
- rule_grad: float32 [16, 2048, 200], P('blk', 'grp')
The draws below stay inside these ranges and needn't reach their ends.
All inputs are finite; a program needn't handle non-finite values.
Results may differ from the reference program's by a relative error of at most 0.01.
Values may be sent and summed in bfloat16 or wider, within the bound.
No kernel may reach another device: no remote copies, remote signals or barrier semaphores. Data moves between devices by JAX's collectives and lax.ppermute only.
A program may use at most 128 MiB of HBM per device.

```python
import math
import jax
import jax.numpy as jnp
from jax import lax

K = 512
F = 2048
REG = 200
HOUR_BLK = 16
PATHS = 128
HOURS = 256
N_BLK = 16


def levels(own_key, shape, pieces, low, largest):
    def one(position, shards_of):
        heights = jax.random.uniform(jax.random.fold_in(jax.random.fold_in(own_key, 6), position), (shards_of,), jnp.float32, low / len(pieces), largest / len(pieces))
        return jnp.repeat(jnp.exp(heights), shape[position] // shards_of).reshape((-1,) + (1,) * (len(shape) - position - 1))

    level = one(*pieces[0])
    for cut in pieces[1:]:
        level = level * one(*cut)
    return level


def bell_draw(own_key, shape, spread, reach, split=(), held_as=jnp.bfloat16):
    result = spread * jax.random.normal(own_key, shape, jnp.float32)
    if split:
        result = result * levels(own_key, shape, split, -0.22, 0.18)
    return jnp.clip(result, -reach, reach).astype(held_as)


def setup_inputs(seed: int = 0) -> dict:
    streams_of = jax.random.split(jax.random.key(seed), 6)
    factors = bell_draw(streams_of[0], (PATHS, HOURS, K), 1.0, 6.0, ((0, 32),))
    loadings = bell_draw(streams_of[1], (K, F), K ** -0.5, 0.25)
    netload_map = bell_draw(streams_of[2], (K, REG), K ** -0.5, 0.25)
    rule_weights = bell_draw(streams_of[3], (N_BLK, F, REG), F ** -0.5, 0.125, ((0, 16),))
    rule_bias = bell_draw(streams_of[4], (N_BLK, REG), 0.5, 3.0, ((0, 16),), jnp.float32)
    return dict(factors=factors, loadings=loadings, netload_map=netload_map, rule_weights=rule_weights, rule_bias=rule_bias)


def reference(factors, loadings, netload_map, rule_weights, rule_bias):
    row_scale = 1.0 / math.sqrt(PATHS * HOUR_BLK)

    def one_block(index):
        start = index * HOUR_BLK
        shocks = lax.dynamic_slice_in_dim(factors, start, HOUR_BLK, 1)
        shocks = jnp.swapaxes(shocks, 0, 1).reshape(HOUR_BLK * PATHS, K)
        features = jnp.tanh(jnp.dot(shocks, loadings, preferred_element_type=jnp.float32)).astype(jnp.bfloat16)
        net_load = jnp.dot(shocks, netload_map, preferred_element_type=jnp.float32).astype(jnp.bfloat16)
        weights = lax.dynamic_index_in_dim(rule_weights, index, 0, keepdims=False)
        offsets = lax.dynamic_index_in_dim(rule_bias, index, 0, keepdims=False)
        dispatch = jnp.dot(features, weights, preferred_element_type=jnp.float32) + offsets
        shortfall = net_load.astype(jnp.float32) - dispatch
        slopes = (-4.0 * jax.nn.sigmoid(shortfall) + jax.nn.sigmoid(-shortfall) + 0.25 * dispatch).astype(jnp.bfloat16)
        grad_block = jnp.dot(features.T, slopes, preferred_element_type=jnp.float32) * row_scale
        return (dispatch.astype(jnp.bfloat16).reshape(HOUR_BLK, PATHS, REG), grad_block)
    decisions, grads = lax.map(one_block, jnp.arange(N_BLK, dtype=jnp.int32))
    return (decisions.reshape(HOURS, PATHS, REG), grads)
```

```python
import functools
import math

import jax
import jax.numpy as jnp
from jax import lax
from jax.experimental import pallas as pl
from jax.experimental.pallas import tpu as pltpu
from jax.sharding import PartitionSpec as P

F32 = jnp.float32
BF16 = jnp.bfloat16
LANES = 128


def dot(a, b, ca, cb):
    return lax.dot_general(a, b, (((ca,), (cb,)), ((), ())), preferred_element_type=F32)


def block_of(size, target):
    while size % target:
        target //= 2
    return target


def rule_kernel(
    groups, hour_blk, row_scale,
    x_ref, load_ref, net_ref, weight_ref, bias_ref,
    dec_ref, send_ref, own_ref,
    feat, slope, disp,
):
    rows, width_f = feat.shape
    regions = weight_ref.shape[0]
    share = width_f // groups
    paths = rows // hour_blk
    row_step = block_of(rows, 256)
    feat_step = block_of(width_f, 512)
    cuts = [(c, min(LANES, regions - c)) for c in range(0, regions, LANES)]
    for r in range(0, rows, row_step):
        here = pl.ds(r, row_step)
        x = x_ref[here, :]
        for c in range(0, width_f, feat_step):
            z = jnp.dot(x, load_ref[:, pl.ds(c, feat_step)], preferred_element_type=F32)
            feat[here, pl.ds(c, feat_step)] = jnp.tanh(z).astype(BF16)
        net = dot(x, net_ref[...], 1, 1).astype(BF16).astype(F32)
        d = dot(feat[here, :], weight_ref[...], 1, 1) + bias_ref[...]
        for i, (c, w) in enumerate(cuts):
            disp[i, here, pl.ds(0, w)] = d[:, c : c + w]
        slope[here, :] = (-1.5 - 2.5 * jnp.tanh(0.5 * (net - d)) + 0.25 * d).astype(BF16)
    for h in range(hour_blk):
        for i, (c, w) in enumerate(cuts):
            dec_ref[h, :, pl.ds(c, w)] = disp[i, pl.ds(h, paths, stride=hour_blk), :][:, :w].astype(BF16)
    mine = lax.axis_index("grp")
    s = slope[...]
    grad_step = block_of(share, 512)
    for step in range(1, groups + 1):
        owner = lax.rem(mine + step, groups)
        for c in range(0, share, grad_step):
            at = pl.ds(pl.multiple_of(owner * share + c, LANES), grad_step)
            g = dot(s, feat[:, at], 0, 0) * row_scale
            if step < groups:
                send_ref[step - 1, :, pl.ds(c, grad_step)] = g.astype(BF16)
            else:
                own_ref[:, pl.ds(c, grad_step)] = g


def body(factors, loadings, netload_map, rule_weights, rule_bias):
    blocks = lax.axis_size("blk")
    groups = lax.axis_size("grp")
    path_dev, hours, width_k = factors.shape
    width_f = loadings.shape[1]
    regions = netload_map.shape[1]
    hour_blk = hours // blocks
    paths = path_dev * blocks
    rows = paths * hour_blk
    share = width_f // groups
    row_scale = 1.0 / math.sqrt(groups * rows)
    ordered = factors.reshape(path_dev, blocks, hour_blk, width_k).swapaxes(0, 1)
    ordered = ordered.reshape(blocks, path_dev * hour_blk, width_k)
    shocks = lax.all_to_all(ordered, "blk", split_axis=0, concat_axis=0, tiled=True)
    vmem = pl.BlockSpec(memory_space=pltpu.VMEM)
    decisions, send, own = pl.pallas_call(
        functools.partial(rule_kernel, groups, hour_blk, row_scale),
        out_shape=(
            jax.ShapeDtypeStruct((hour_blk, paths, regions), BF16),
            jax.ShapeDtypeStruct((max(groups - 1, 1), regions, share), BF16),
            jax.ShapeDtypeStruct((regions, share), F32),
        ),
        in_specs=[vmem] * 5,
        out_specs=[vmem] * 3,
        scratch_shapes=[
            pltpu.VMEM((rows, width_f), BF16),
            pltpu.VMEM((rows, regions), BF16),
            pltpu.VMEM((pl.cdiv(regions, LANES), rows, LANES), F32),
        ],
        compiler_params=pltpu.CompilerParams(vmem_limit_bytes=40 << 20),
        name="rules",
    )(
        shocks.reshape(rows, width_k),
        loadings,
        netload_map.T,
        rule_weights[0].T,
        rule_bias,
    )
    grad = own
    for step in range(1, groups):
        pairs = [(g, (g + step) % groups) for g in range(groups)]
        grad = grad + lax.ppermute(send[step - 1], "grp", pairs).astype(F32)
    return decisions, grad.T[None]


def solution(mesh):
    return jax.shard_map(
        body,
        mesh=mesh,
        in_specs=(P(("grp", "blk"), None, None), P(), P(), P("blk", None, None), P("blk", None)),
        out_specs=(P("blk", "grp", None), P("blk", "grp", None)),
        check_vma=False,
    )
```

```python
import functools
import math

import jax
import jax.numpy as jnp
from jax import lax
from jax.experimental import pallas as pl
from jax.experimental.pallas import tpu as pltpu
from jax.sharding import PartitionSpec as P

F32 = jnp.float32
BF16 = jnp.bfloat16
LANES = 128
PLANE = 4


def dot(a, b, ca, cb):
    return lax.dot_general(a, b, (((ca,), (cb,)), ((), ())), preferred_element_type=F32)


def block_of(size, target):
    while size % target:
        target //= 2
    return target


def cuts_of(regions):
    return [(i, c, min(LANES, regions - c)) for i, c in enumerate(range(0, regions, LANES))]


def place_of_device():
    me = lax.axis_index("blk")
    return me // PLANE, me % PLANE


def run_copies(moves, sem):
    copies = [pltpu.make_async_copy(a, b, sem.at[i]) for i, (a, b) in enumerate(moves)]
    for c in copies:
        c.start()
    for c in copies:
        c.wait()


def units_of(slow, path_dev, n1):
    half = slow // 2
    counts = [path_dev if dz < half else path_dev - n1 for dz in range(slow)]
    return counts, [sum(counts[:dz]) for dz in range(slow)]


def pack_far_kernel(n1, x_ref, *refs):
    outs, sem = refs[:-1], refs[-1]
    z, _ = place_of_device()
    half = len(outs)
    run_copies([(x_ref.at[pl.ds(0, n1), z ^ (half + i)], out) for i, out in enumerate(outs)], sem)


def pack_near_kernel(n1, x_ref, after_ref, *refs):
    nears, sem = refs[:-1], refs[-1]
    z, f = place_of_device()
    path_dev, slow = x_ref.shape[:2]
    counts, offs = units_of(slow, path_dev, n1)
    run_copies(
        [
            (x_ref.at[pl.ds(path_dev - counts[dz], counts[dz]), z ^ dz, f ^ d], near.at[pl.ds(offs[dz], counts[dz])])
            for dz in range(slow) for d, near in enumerate(nears)
        ],
        sem,
    )


def turn_near_kernel(offs, *refs):
    nears, outs = refs[:PLANE], refs[PLANE:]
    for out, off in zip(outs, offs):
        for d, near in enumerate(nears):
            out[d] = near[pl.ds(off, out.shape[1])]


def turn_far_kernel(half, *refs):
    fars, outs = refs[:half], refs[-PLANE:]
    _, f = place_of_device()
    for d, out in enumerate(outs):
        for i, far in enumerate(fars):
            out[i] = far[:, f ^ d]


def front(x, weights, feat, slope, at):
    load_ref, net_ref, weight_ref, bias_ref = weights
    here = pl.ds(at, x.shape[0])
    width_f = load_ref.shape[1]
    step = block_of(width_f, 512)
    for c in range(0, width_f, step):
        y = jnp.dot(x, load_ref[:, pl.ds(c, step)], preferred_element_type=F32)
        feat[here, pl.ds(c, step)] = jnp.tanh(y).astype(BF16)
    net = dot(x, net_ref[...], 1, 1).astype(BF16).astype(F32)
    d = dot(feat[here, :], weight_ref[...], 1, 1) + bias_ref[...]
    slope[here, :] = (-1.5 - 2.5 * jnp.tanh(0.5 * (net - d)) + 0.25 * d).astype(BF16)
    return d


def rules(pieces, path_dev, weights, disp_ref, feat, slope):
    z, f = place_of_device()
    at = 0
    while pieces:
        batch, size = [], 0
        while pieces and (not batch or size + math.prod(pieces[0][0].shape[:2]) <= 256):
            batch.append(pieces[0])
            size += math.prod(pieces[0][0].shape[:2])
            pieces = pieces[1:]
        x = jnp.concatenate([r[...].reshape(-1, r.shape[-1]) for r, _, _, _ in batch], 0)
        d = front(x, weights, feat, slope, at)
        row = 0
        for r, first, dz, df in batch:
            n, hour_blk = r.shape[:2]
            source = (z ^ dz) * PLANE + (f ^ df)
            start = pl.multiple_of((source * path_dev + first) * hour_blk, 16)
            for i, c, w in cuts_of(d.shape[1]):
                disp_ref[i, pl.ds(start, n * hour_blk), pl.ds(0, w)] = d[row : row + n * hour_blk, c : c + w]
            row += n * hour_blk
        at += size


def grad_parts(groups, slope, feat, steps):
    share = feat.shape[1] // groups
    mine = lax.axis_index("grp")
    s = slope[...]
    width = block_of(share, 512)
    for step in steps:
        owner = lax.rem(mine + step, groups)
        for c in range(0, share, width):
            at = pl.ds(pl.multiple_of(owner * share + c, LANES), width)
            yield step - 1, pl.ds(c, width), dot(s, feat[:, at], 0, 0)


def near_pieces(nears, path_dev):
    return [(near.at[pl.ds(0, path_dev)], 0, 0, d) for d, near in enumerate(nears)]


def plane_pieces(planes, dzs, first):
    return [(plane.at[d], first, dz, d) for plane, dz in zip(planes, dzs) for d in range(PLANE)]


def far_pieces(fars, half):
    return [(far.at[i], 0, half + i, d) for d, far in enumerate(fars) for i in range(half)]


def first_kernel(groups, path_dev, *refs):
    nears, weights, (disp_ref, acc_ref, slope, feat) = refs[:PLANE], refs[PLANE : PLANE + 4], refs[PLANE + 4 :]
    rules(near_pieces(nears, path_dev), path_dev, weights, disp_ref, feat, slope)
    for i, at, g in grad_parts(groups, slope, feat, range(1, groups + 1)):
        acc_ref[i, :, at] = g


def middle_kernel(groups, path_dev, half, *refs):
    k = half - 1
    planes, fars, refs = refs[:k], refs[k : k + PLANE], refs[k + PLANE :]
    weights, (disp_in, acc_in, disp_ref, acc_ref, slope, feat) = refs[:4], refs[4:]
    pieces = plane_pieces(planes, range(1, half), 0) + far_pieces(fars, half)
    rules(pieces, path_dev, weights, disp_ref, feat, slope)
    for i, at, g in grad_parts(groups, slope, feat, range(1, groups + 1)):
        acc_ref[i, :, at] = g + acc_in[i, :, at]


def last_kernel(groups, path_dev, half, n1, row_scale, *refs):
    planes, weights, refs = refs[:half], refs[half : half + 4], refs[half + 4 :]
    disp_in, acc_ref, disp_ref, send_ref, own_feat, slope, feat = refs
    rules(plane_pieces(planes, range(half, 2 * half), n1), path_dev, weights, disp_ref, feat, slope)
    for i, at, g in grad_parts(groups, slope, feat, range(1, groups)):
        send_ref[i, :, at] = ((g + acc_ref[i, :, at]) * row_scale).astype(BF16)
    share = own_feat.shape[1]
    own_feat[...] = feat[:, pl.ds(pl.multiple_of(lax.axis_index("grp") * share, LANES), share)]


def finish_kernel(row_scale, own_feat, slope, acc_ref, disp_ref, dec_ref, own_ref):
    last = acc_ref.shape[0] - 1
    share = own_feat.shape[1]
    hour_blk, paths, regions = dec_ref.shape
    s = slope[...]
    width = block_of(share, 512)
    for c in range(0, share, width):
        at = pl.ds(c, width)
        own_ref[:, at] = (dot(s, own_feat[:, at], 0, 0) + acc_ref[last, :, at]) * row_scale
    for h in range(hour_blk):
        for i, c, w in cuts_of(regions):
            dec_ref[h, :, pl.ds(c, w)] = disp_ref[i, pl.ds(h, paths, stride=hour_blk), :][:, :w].astype(BF16)


def call(kernel, name, outs, operands, scratch=(), flops=0, aliases=None, in_hbm=0):
    vmem = pl.BlockSpec(memory_space=pltpu.VMEM)
    hbm = pl.BlockSpec(memory_space=pl.ANY)
    moved = sum(math.prod(a.shape) * a.dtype.itemsize for a in [*operands, *outs])
    return pl.pallas_call(
        kernel,
        out_shape=tuple(outs),
        in_specs=[hbm] * in_hbm + [vmem] * (len(operands) - in_hbm),
        out_specs=[vmem] * len(outs),
        scratch_shapes=list(scratch),
        input_output_aliases=aliases or {},
        compiler_params=pltpu.CompilerParams(vmem_limit_bytes=16 << 20),
        cost_estimate=pl.CostEstimate(flops=0, bytes_accessed=0, transcendentals=0),
        name=name,
    )(*operands)


def body(factors, loadings, netload_map, rule_weights, rule_bias):
    blocks = lax.axis_size("blk")
    groups = lax.axis_size("grp")
    path_dev, hours, width_k = factors.shape
    width_f = loadings.shape[1]
    regions = netload_map.shape[1]
    hour_blk = hours // blocks
    paths = path_dev * blocks
    rows = paths * hour_blk
    share = width_f // groups
    slow = blocks // PLANE
    half = slow // 2
    row_scale = 1.0 / math.sqrt(groups * rows)
    n1 = path_dev // 2
    n2 = path_dev - n1
    counts, offs = units_of(slow, path_dev, n1)

    def hop(x, distance):
        return lax.ppermute(x, "blk", [(i, i ^ distance) for i in range(blocks)])

    def bf(*shape):
        return jax.ShapeDtypeStruct(shape, BF16)

    def f32(*shape):
        return jax.ShapeDtypeStruct(shape, F32)

    def sems(n):
        return [pltpu.SemaphoreType.DMA((n,))]

    view = factors.reshape(path_dev, slow, PLANE, hour_blk, width_k)
    fars = call(
        functools.partial(pack_far_kernel, n1), "pack_far",
        [bf(n1, PLANE, hour_blk, width_k)] * half, [view], sems(half), in_hbm=1,
    )
    nears = call(
        functools.partial(pack_near_kernel, n1), "pack_near",
        [bf(sum(counts), hour_blk, width_k)] * PLANE, [view, fars[0]], sems(slow * PLANE), in_hbm=2,
    )
    fars = [hop(x, (half + i) * PLANE) for i, x in enumerate(fars)]
    nears = [hop(x, d) if d else x for d, x in enumerate(nears)]
    planes = call(
        functools.partial(turn_near_kernel, offs[1:]), "turn_near",
        [bf(PLANE, counts[dz], hour_blk, width_k) for dz in range(1, slow)], nears,
    )
    fars = call(
        functools.partial(turn_far_kernel, half), "turn_far",
        [bf(half, n1, hour_blk, width_k)] * PLANE, fars,
    )
    planes = [hop(x, dz * PLANE) for dz, x in zip(range(1, slow), planes)]
    fars = [hop(x, d) if d else x for d, x in enumerate(fars)]

    weights = (loadings, netload_map.T, rule_weights[0].T, rule_bias)
    disp_shape = f32(pl.cdiv(regions, LANES), rows, LANES)
    acc_shape = f32(groups, regions, share)
    row_flops = 2.0 * (width_k * width_f + width_k * regions + 2 * width_f * regions)

    def scratch(n):
        return [pltpu.VMEM((n, regions), BF16), pltpu.VMEM((n, width_f), BF16)]

    n = PLANE * path_dev * hour_blk
    disp, acc = call(
        functools.partial(first_kernel, groups, path_dev), "rules_first",
        [disp_shape, acc_shape], [*nears, *weights], scratch(n), n * row_flops,
    )
    n = (half - 1) * PLANE * path_dev * hour_blk + half * PLANE * n1 * hour_blk
    k = half - 1 + PLANE + 4
    disp, acc = call(
        functools.partial(middle_kernel, groups, path_dev, half), "rules_middle",
        [disp_shape, acc_shape], [*planes[: half - 1], *fars, *weights, disp, acc],
        scratch(n), n * row_flops, {k: 0, k + 1: 1},
    )
    n = half * PLANE * n2 * hour_blk
    disp, send, own_feat, slope = call(
        functools.partial(last_kernel, groups, path_dev, half, n1, row_scale), "rules_last",
        [disp_shape, bf(max(groups - 1, 1), regions, share), bf(n, share), bf(n, regions)],
        [*planes[half - 1 :], *weights, disp, acc],
        [pltpu.VMEM((n, width_f), BF16)], n * row_flops, {half + 4: 0},
    )
    decisions, grad = call(
        functools.partial(finish_kernel, row_scale), "rules_finish",
        [bf(hour_blk, paths, regions), f32(regions, share)],
        [own_feat, slope, acc, disp], [], 2.0 * n * share * regions,
    )
    for step in range(1, groups):
        pairs = [(g, (g + step) % groups) for g in range(groups)]
        grad = grad + lax.ppermute(send[step - 1], "grp", pairs).astype(F32)
    return decisions, grad.T[None]


def solution(mesh):
    return jax.shard_map(
        body,
        mesh=mesh,
        in_specs=(P(("grp", "blk"), None, None), P(), P(), P("blk", None, None), P("blk", None)),
        out_specs=(P("blk", "grp", None), P("blk", "grp", None)),
        check_vma=False,
    )
```

```python
import functools
import math

import jax
import jax.numpy as jnp
from jax import lax
from jax.experimental import pallas as pl
from jax.experimental.pallas import tpu as pltpu
from jax.sharding import PartitionSpec as P

F32 = jnp.float32
BF16 = jnp.bfloat16
LANES = 128
PLANE = 4


def dot(a, b, ca, cb):
    return lax.dot_general(a, b, (((ca,), (cb,)), ((), ())), preferred_element_type=F32)


def block_of(size, target):
    while size % target:
        target //= 2
    return target


def cuts_of(regions):
    return [(i, c, min(LANES, regions - c)) for i, c in enumerate(range(0, regions, LANES))]


def run_copies(moves, sem):
    copies = [pltpu.make_async_copy(a, b, sem.at[i]) for i, (a, b) in enumerate(moves)]
    for c in copies:
        c.start()
    for c in copies:
        c.wait()


def flips(groups, blocks):
    return groups % 2 == 0 and blocks == PLANE * PLANE


def digits(cfg):
    groups, blocks = cfg
    me = lax.axis_index("blk")
    hi, lo = me // PLANE, me % PLANE
    if not flips(groups, blocks):
        return hi, lo, None
    flip = lax.axis_index("grp") % 2
    return jnp.where(flip, lo, hi), jnp.where(flip, hi, lo), flip


def block_id(a, b, flip):
    straight = a * PLANE + b
    return straight if flip is None else jnp.where(flip, b * PLANE + a, straight)


def far_first(k, radix):
    return radix - k if k else 0


def pack_kernel(cfg, x_ref, *outs):
    a, _, flip = digits(cfg)
    for k, out in enumerate(outs):
        for b in range(PLANE):
            out[b] = x_ref[:, block_id(a ^ far_first(k, len(outs)), b, flip)]


def front(x, weights, feat, slope, at):
    load_ref, net_ref, weight_ref, bias_ref = weights
    here = pl.ds(at, x.shape[0])
    width_f = load_ref.shape[1]
    step = block_of(width_f, 512)
    for c in range(0, width_f, step):
        y = jnp.dot(x, load_ref[:, pl.ds(c, step)], preferred_element_type=F32)
        feat[here, pl.ds(c, step)] = jnp.tanh(y).astype(BF16)
    net = dot(x, net_ref[...], 1, 1).astype(BF16).astype(F32)
    d = dot(feat[here, :], weight_ref[...], 1, 1) + bias_ref[...]
    slope[here, :] = (-1.5 - 2.5 * jnp.tanh(0.5 * (net - d)) + 0.25 * d).astype(BF16)
    return d


def rules(cfg, arrived, weights, disp_ref, feat, slope):
    a, b, flip = digits(cfg)
    radix = len(arrived[0][1])
    path_dev, hour_blk, width_k = arrived[0][1][0].shape
    piece = path_dev * hour_blk
    per = block_of(radix, max(256 // piece, 1))
    at = 0
    for m, parts in arrived:
        for k in range(0, radix, per):
            x = jnp.concatenate([p[...].reshape(piece, width_k) for p in parts[k : k + per]], 0)
            d = front(x, weights, feat, slope, at)
            for i in range(per):
                start = pl.multiple_of(block_id(a ^ far_first(k + i, radix), b ^ m, flip) * piece, 16)
                for j, c, w in cuts_of(d.shape[1]):
                    disp_ref[j, pl.ds(start, piece), pl.ds(0, w)] = d[i * piece : (i + 1) * piece, c : c + w]
            at += per * piece


def grad_parts(groups, slope, feat, steps):
    share = feat.shape[1] // groups
    mine = lax.axis_index("grp")
    s = slope[...]
    width = block_of(share, 512)
    for step in steps:
        owner = lax.rem(mine + step, groups)
        for c in range(0, share, width):
            at = pl.ds(pl.multiple_of(owner * share + c, LANES), width)
            yield step - 1, pl.ds(c, width), dot(s, feat[:, at], 0, 0)


def load_kernel(cfg, *refs):
    k = (len(refs) - 1) // 2
    _, _, flip = digits(cfg)

    def load():
        run_copies(list(zip(refs[:k], refs[k:-1])), refs[-1])

    if flip is None:
        load()
    else:
        pl.when(flip == 0)(load)


def own_digit(cfg, parts, weights, disp_ref, acc_ref, slope, feat):
    _, b, _ = digits(cfg)
    rules(cfg, [(0, [p.at[b] for p in parts])], weights, disp_ref, feat, slope)
    for i, at, g in grad_parts(cfg[0], slope, feat, range(1, cfg[0] + 1)):
        acc_ref[i, :, at] = g


def turn_kernel(cfg, radix, *refs):
    raw, refs = refs[:4], refs[4:]
    parts, refs = refs[:radix], refs[radix + 4 :]
    weights, outs, (disp_ref, acc_ref, slope, feat, sem) = refs[:4], refs[4:-5], refs[-5:]
    _, b, flip = digits(cfg)
    if flip is not None:
        @pl.when(flip == 1)
        def _():
            run_copies(list(zip(raw, weights)), sem)
            own_digit(cfg, parts, weights, disp_ref, acc_ref, slope, feat)
    for m, out in enumerate(outs, 1):
        for k, part in enumerate(parts):
            out[k] = part[b ^ m]


def first_kernel(cfg, radix, *refs):
    parts, weights, refs = refs[:radix], refs[radix : radix + 4], refs[radix + 4 :]
    disp_in, acc_in, disp_ref, acc_ref, slope, feat = refs
    _, _, flip = digits(cfg)
    if flip is None:
        own_digit(cfg, parts, weights, disp_ref, acc_ref, slope, feat)
    else:
        @pl.when(flip == 0)
        def _():
            own_digit(cfg, parts, weights, disp_ref, acc_ref, slope, feat)


def middle_kernel(cfg, ms, at, *refs):
    k = len(ms)
    xs, weights, refs = refs[:k], refs[k : k + 4], refs[k + 4 :]
    disp_ref, feat, slope = refs[-3:]
    rows = sum(math.prod(x.shape[:-1]) for x in xs)
    here = pl.ds(at, rows)
    rules(
        cfg, [(m, [x.at[i] for i in range(x.shape[0])]) for m, x in zip(ms, xs)], weights, disp_ref,
        feat.at[here], slope.at[here],
    )


def last_kernel(cfg, ms, at, row_scale, *refs):
    acc_ref, send_ref, refs = refs[0], refs[-4], refs[1:-4] + refs[-3:]
    middle_kernel(cfg, ms, at, *refs)
    _, feat, slope = refs[-3:]
    for i, cols, g in grad_parts(cfg[0], slope, feat, range(1, cfg[0])):
        send_ref[i, :, cols] = ((g + acc_ref[i, :, cols]) * row_scale).astype(BF16)


def finish_kernel(groups, row_scale, feat, slope, acc_ref, disp_ref, dec_ref, own_ref):
    hour_blk, paths, regions = dec_ref.shape
    for i, cols, g in grad_parts(groups, slope, feat, [groups]):
        own_ref[:, cols] = (g + acc_ref[i, :, cols]) * row_scale
    for h in range(hour_blk):
        for i, c, w in cuts_of(regions):
            dec_ref[h, :, pl.ds(c, w)] = disp_ref[i, pl.ds(h, paths, stride=hour_blk), :][:, :w].astype(BF16)


def call(kernel, name, outs, operands, scratch=(), aliases=None, in_hbm=0):
    vmem = pl.BlockSpec(memory_space=pltpu.VMEM)
    hbm = pl.BlockSpec(memory_space=pl.ANY)
    return pl.pallas_call(
        kernel,
        out_shape=tuple(outs),
        in_specs=[hbm] * in_hbm + [vmem] * (len(operands) - in_hbm),
        out_specs=[vmem] * len(outs),
        scratch_shapes=list(scratch),
        input_output_aliases=aliases or {},
        compiler_params=pltpu.CompilerParams(vmem_limit_bytes=16 << 20),
        cost_estimate=pl.CostEstimate(flops=0, bytes_accessed=0, transcendentals=0),
        name=name,
    )(*operands)


def body(factors, loadings, netload_map, rule_weights, rule_bias):
    blocks = lax.axis_size("blk")
    groups = lax.axis_size("grp")
    path_dev, hours, width_k = factors.shape
    width_f = loadings.shape[1]
    regions = netload_map.shape[1]
    hour_blk = hours // blocks
    paths = path_dev * blocks
    rows = paths * hour_blk
    share = width_f // groups
    radix = blocks // PLANE
    row_scale = 1.0 / math.sqrt(groups * rows)
    cfg = (groups, blocks)

    def bf(*shape):
        return jax.ShapeDtypeStruct(shape, BF16)

    def f32(*shape):
        return jax.ShapeDtypeStruct(shape, F32)

    def hop(x, straight, flipped):
        pairs = []
        for g in range(groups):
            distance = flipped if flips(groups, blocks) and g % 2 else straight
            pairs += [(g * blocks + i, g * blocks + (i ^ distance)) for i in range(blocks)]
        return lax.ppermute(x, ("grp", "blk"), pairs)

    parts = call(
        functools.partial(pack_kernel, cfg), "pack",
        [bf(PLANE, path_dev, hour_blk, width_k)] * radix,
        [factors.reshape(path_dev, blocks, hour_blk, width_k)],
    )
    dist = [far_first(k, radix) for k in range(radix)]
    parts = [hop(x, d * PLANE, d) if d else x for d, x in zip(dist, parts)]
    weights = (loadings, netload_map.T, rule_weights[0].T, rule_bias)
    raw = weights
    weights = call(
        functools.partial(load_kernel, cfg), "load", [jax.ShapeDtypeStruct(w.shape, w.dtype) for w in weights], weights,
        [pltpu.SemaphoreType.DMA((len(weights),))], in_hbm=len(weights),
    )
    disp_shape = f32(pl.cdiv(regions, LANES), rows, LANES)
    acc_shape = f32(groups, regions, share)

    def scratch(ms):
        n = len(ms) * rows // PLANE
        return [pltpu.VMEM((n, regions), BF16), pltpu.VMEM((n, width_f), BF16)]

    def inputs(ms):
        return [arrived[m] for m in ms]

    middle, last = [[1], [2]], [3]
    *turned, disp, acc = call(
        functools.partial(turn_kernel, cfg, radix), "turn",
        [jax.ShapeDtypeStruct(w.shape, w.dtype) for w in weights]
        + [bf(radix, path_dev, hour_blk, width_k)] * (PLANE - 1) + [disp_shape, acc_shape],
        [*raw, *parts, *weights], scratch([0]) + [pltpu.SemaphoreType.DMA((4,))],
        {4 + radix + i: i for i in range(4)}, in_hbm=4,
    )
    weights, turned = turned[:4], turned[4:]
    arrived = {m: hop(x, m, m * PLANE) for m, x in enumerate(turned, 1)}
    k = radix + 4
    disp, acc = call(
        functools.partial(first_kernel, cfg, radix), "rules_first",
        [disp_shape, acc_shape], [*parts, *weights, disp, acc], scratch([0]), {k: 0, k + 1: 1},
    )
    n = rows // PLANE
    late = (PLANE - 1) * n
    shapes = [disp_shape, bf(late, width_f), bf(late, regions)]
    state, at = [disp], 0
    for ms in middle:
        k = len(ms) + 4
        state = call(
            functools.partial(middle_kernel, cfg, ms, at), "rules_middle", shapes,
            [*inputs(ms), *weights, *state], aliases={k + i: i for i in range(len(state))},
        )
        at += len(ms) * n
    k = len(last) + 5
    send, disp, feat, slope = call(
        functools.partial(last_kernel, cfg, last, at, row_scale), "rules_last",
        [bf(max(groups - 1, 1), regions, share), *shapes],
        [acc, *inputs(last), *weights, *state], aliases={k + i: 1 + i for i in range(len(state))},
    )
    decisions, grad = call(
        functools.partial(finish_kernel, groups, row_scale), "rules_finish",
        [bf(hour_blk, paths, regions), f32(regions, share)], [feat, slope, acc, disp],
    )
    for step in range(1, groups):
        pairs = [(g, (g + step) % groups) for g in range(groups)]
        grad = grad + lax.ppermute(send[step - 1], "grp", pairs).astype(F32)
    return decisions, grad.T[None]


def solution(mesh):
    return jax.shard_map(
        body,
        mesh=mesh,
        in_specs=(P(("grp", "blk"), None, None), P(), P(), P("blk", None, None), P("blk", None)),
        out_specs=(P("blk", "grp", None), P("blk", "grp", None)),
        check_vma=False,
    )
```

```python
import functools
import math

import jax
import jax.numpy as jnp
from jax import lax
from jax.experimental import pallas as pl
from jax.experimental.pallas import tpu as pltpu
from jax.sharding import PartitionSpec as P

F32 = jnp.float32
BF16 = jnp.bfloat16
LANES = 128
PLANE = 4


def dot(a, b, ca, cb):
    return lax.dot_general(a, b, (((ca,), (cb,)), ((), ())), preferred_element_type=F32)


def block_of(size, target):
    while size % target:
        target //= 2
    return target


def cuts_of(regions):
    return [(i, c, min(LANES, regions - c)) for i, c in enumerate(range(0, regions, LANES))]


def run_copies(moves, sem):
    copies = [pltpu.make_async_copy(a, b, sem.at[i]) for i, (a, b) in enumerate(moves)]
    for c in copies:
        c.start()
    for c in copies:
        c.wait()


def flips(groups, blocks):
    return groups % 2 == 0 and blocks == PLANE * PLANE


def digits(cfg):
    groups, blocks = cfg
    me = lax.axis_index("blk")
    hi, lo = me // PLANE, me % PLANE
    if not flips(groups, blocks):
        return hi, lo, None
    flip = lax.axis_index("grp") % 2
    return jnp.where(flip, lo, hi), jnp.where(flip, hi, lo), flip


def block_id(a, b, flip):
    straight = a * PLANE + b
    return straight if flip is None else jnp.where(flip, b * PLANE + a, straight)


FIRST_HOPS = (2, 1, 3)
SECOND_HOPS = (2, 1, 3)
FLIPPED_SECOND_HOPS = (1, 2, 3)


def first_distance(k, radix):
    if not k:
        return 0
    return FIRST_HOPS[k - 1] if radix == PLANE else radix - k


def second_distance(m, flip):
    if not m:
        return 0
    straight, flipped = SECOND_HOPS[m - 1], FLIPPED_SECOND_HOPS[m - 1]
    return straight if flip is None else jnp.where(flip, flipped, straight)


def pack_kernel(cfg, x_ref, *outs):
    a, _, flip = digits(cfg)
    for k, out in enumerate(outs):
        for b in range(PLANE):
            out[b] = x_ref[:, block_id(a ^ first_distance(k, len(outs)), b, flip)]


def front(x, weights, feat, slope, at):
    load_ref, net_ref, weight_ref, bias_ref = weights
    here = pl.ds(at, x.shape[0])
    width_f = load_ref.shape[1]
    step = block_of(width_f, 512)
    for c in range(0, width_f, step):
        y = jnp.dot(x, load_ref[:, pl.ds(c, step)], preferred_element_type=F32)
        feat[here, pl.ds(c, step)] = jnp.tanh(y).astype(BF16)
    net = dot(x, net_ref[...], 1, 1).astype(BF16).astype(F32)
    d = dot(feat[here, :], weight_ref[...], 1, 1) + bias_ref[...]
    slope[here, :] = (-1.5 - 2.5 * jnp.tanh(0.5 * (net - d)) + 0.25 * d).astype(BF16)
    return d


def rules(cfg, arrived, weights, disp_ref, feat, slope):
    a, b, flip = digits(cfg)
    radix = len(arrived[0][1])
    path_dev, hour_blk, width_k = arrived[0][1][0].shape
    piece = path_dev * hour_blk
    per = block_of(radix, max(256 // piece, 1))
    at = 0
    for m, parts in arrived:
        for k in range(0, radix, per):
            x = jnp.concatenate([p[...].reshape(piece, width_k) for p in parts[k : k + per]], 0)
            d = front(x, weights, feat, slope, at)
            for i in range(per):
                start = pl.multiple_of(block_id(a ^ first_distance(k + i, radix), b ^ second_distance(m, flip), flip) * piece, 16)
                for j, c, w in cuts_of(d.shape[1]):
                    disp_ref[j, pl.ds(start, piece), pl.ds(0, w)] = d[i * piece : (i + 1) * piece, c : c + w]
            at += per * piece


def grad_parts(groups, slope, feat, steps):
    share = feat.shape[1] // groups
    mine = lax.axis_index("grp")
    s = slope[...]
    width = block_of(share, 512)
    for step in steps:
        owner = lax.rem(mine + step, groups)
        for c in range(0, share, width):
            at = pl.ds(pl.multiple_of(owner * share + c, LANES), width)
            yield step - 1, pl.ds(c, width), dot(s, feat[:, at], 0, 0)


def load_kernel(*refs):
    k = (len(refs) - 1) // 2
    run_copies(list(zip(refs[:k], refs[k:-1])), refs[-1])


def own_digit(cfg, parts, weights, disp_ref, acc_ref, slope, feat):
    _, b, _ = digits(cfg)
    rules(cfg, [(0, [p.at[b] for p in parts])], weights, disp_ref, feat, slope)
    for i, at, g in grad_parts(cfg[0], slope, feat, range(1, cfg[0] + 1)):
        acc_ref[i, :, at] = g


def turn_kernel(cfg, radix, *refs):
    parts, weights, refs = refs[:radix], refs[radix : radix + 4], refs[radix + 4 :]
    outs, (disp_ref, acc_ref, slope, feat) = refs[:-4], refs[-4:]
    _, b, flip = digits(cfg)
    if flip is not None:
        @pl.when(flip == 1)
        def _():
            own_digit(cfg, parts, weights, disp_ref, acc_ref, slope, feat)
    for m, out in enumerate(outs, 1):
        for k, part in enumerate(parts):
            out[k] = part[b ^ second_distance(m, flip)]


def first_kernel(cfg, radix, *refs):
    parts, weights, refs = refs[:radix], refs[radix : radix + 4], refs[radix + 4 :]
    disp_in, acc_in, disp_ref, acc_ref, slope, feat = refs
    _, _, flip = digits(cfg)
    if flip is None:
        own_digit(cfg, parts, weights, disp_ref, acc_ref, slope, feat)
    else:
        @pl.when(flip == 0)
        def _():
            own_digit(cfg, parts, weights, disp_ref, acc_ref, slope, feat)


def gather_kernel(cfg, ms, *refs):
    k = len(ms)
    xs, weights, refs = refs[:k], refs[k : k + 4], refs[k + 4 :]
    disp_in, acc_in, disp_ref, acc_ref, slope, feat = refs
    rules(cfg, [(m, [x.at[i] for i in range(x.shape[0])]) for m, x in zip(ms, xs)], weights, disp_ref, feat, slope)
    for i, cols, g in grad_parts(cfg[0], slope, feat, range(1, cfg[0] + 1)):
        acc_ref[i, :, cols] = g + acc_in[i, :, cols]


def middle_kernel(cfg, ms, at, *refs):
    k = len(ms)
    xs, weights, refs = refs[:k], refs[k : k + 4], refs[k + 4 :]
    disp_ref, feat, slope = refs[-3:]
    rows = sum(math.prod(x.shape[:-1]) for x in xs)
    here = pl.ds(at, rows)
    rules(
        cfg, [(m, [x.at[i] for i in range(x.shape[0])]) for m, x in zip(ms, xs)], weights, disp_ref,
        feat.at[here], slope.at[here],
    )


def last_kernel(cfg, ms, at, row_scale, *refs):
    acc_ref, send_ref, refs = refs[0], refs[-4], refs[1:-4] + refs[-3:]
    middle_kernel(cfg, ms, at, *refs)
    _, feat, slope = refs[-3:]
    for i, cols, g in grad_parts(cfg[0], slope, feat, range(1, cfg[0])):
        send_ref[i, :, cols] = ((g + acc_ref[i, :, cols]) * row_scale).astype(BF16)


def finish_kernel(groups, row_scale, feat, slope, acc_ref, disp_ref, dec_ref, own_ref):
    hour_blk, paths, regions = dec_ref.shape
    for i, cols, g in grad_parts(groups, slope, feat, [groups]):
        own_ref[:, cols] = (g + acc_ref[i, :, cols]) * row_scale
    for h in range(hour_blk):
        for i, c, w in cuts_of(regions):
            dec_ref[h, :, pl.ds(c, w)] = disp_ref[i, pl.ds(h, paths, stride=hour_blk), :][:, :w].astype(BF16)


def call(kernel, name, outs, operands, scratch=(), aliases=None, in_hbm=0):
    vmem = pl.BlockSpec(memory_space=pltpu.VMEM)
    hbm = pl.BlockSpec(memory_space=pl.ANY)
    return pl.pallas_call(
        kernel,
        out_shape=tuple(outs),
        in_specs=[hbm] * in_hbm + [vmem] * (len(operands) - in_hbm),
        out_specs=[vmem] * len(outs),
        scratch_shapes=list(scratch),
        input_output_aliases=aliases or {},
        compiler_params=pltpu.CompilerParams(vmem_limit_bytes=16 << 20),
        cost_estimate=pl.CostEstimate(flops=0, bytes_accessed=0, transcendentals=0),
        name=name,
    )(*operands)


def body(factors, loadings, netload_map, rule_weights, rule_bias):
    blocks = lax.axis_size("blk")
    groups = lax.axis_size("grp")
    path_dev, hours, width_k = factors.shape
    width_f = loadings.shape[1]
    regions = netload_map.shape[1]
    hour_blk = hours // blocks
    paths = path_dev * blocks
    rows = paths * hour_blk
    share = width_f // groups
    radix = blocks // PLANE
    row_scale = 1.0 / math.sqrt(groups * rows)
    cfg = (groups, blocks)

    def bf(*shape):
        return jax.ShapeDtypeStruct(shape, BF16)

    def f32(*shape):
        return jax.ShapeDtypeStruct(shape, F32)

    def hop(x, straight, flipped):
        pairs = []
        for g in range(groups):
            distance = flipped if flips(groups, blocks) and g % 2 else straight
            pairs += [(g * blocks + i, g * blocks + (i ^ distance)) for i in range(blocks)]
        return lax.ppermute(x, ("grp", "blk"), pairs)

    parts = call(
        functools.partial(pack_kernel, cfg), "pack",
        [bf(PLANE, path_dev, hour_blk, width_k)] * radix,
        [factors.reshape(path_dev, blocks, hour_blk, width_k)],
    )
    dist = [first_distance(k, radix) for k in range(radix)]
    parts = [hop(x, d * PLANE, d) if d else x for d, x in zip(dist, parts)]
    weights = (loadings, netload_map.T, rule_weights[0].T, rule_bias)
    weights = call(
        load_kernel, "load", [jax.ShapeDtypeStruct(w.shape, w.dtype) for w in weights], weights,
        [pltpu.SemaphoreType.DMA((len(weights),))], in_hbm=len(weights),
    )
    disp_shape = f32(pl.cdiv(regions, LANES), rows, LANES)
    acc_shape = f32(groups, regions, share)

    def scratch(ms):
        n = len(ms) * rows // PLANE
        return [pltpu.VMEM((n, regions), BF16), pltpu.VMEM((n, width_f), BF16)]

    def inputs(ms):
        return [arrived[m] for m in ms]

    middle, last = [[1], [2]], [3]
    *turned, disp, acc = call(
        functools.partial(turn_kernel, cfg, radix), "turn",
        [bf(radix, path_dev, hour_blk, width_k)] * (PLANE - 1) + [disp_shape, acc_shape],
        [*parts, *weights], scratch([0]),
    )
    arrived = {m: hop(x, SECOND_HOPS[m - 1], FLIPPED_SECOND_HOPS[m - 1] * PLANE) for m, x in enumerate(turned, 1)}
    k = radix + 4
    disp, acc = call(
        functools.partial(first_kernel, cfg, radix), "rules_first",
        [disp_shape, acc_shape], [*parts, *weights, disp, acc], scratch([0]), {k: 0, k + 1: 1},
    )
    n = rows // PLANE
    early, middle = middle[0], middle[1:]
    late = (PLANE - 1 - len(early)) * n
    k = len(early) + 4
    disp, acc = call(
        functools.partial(gather_kernel, cfg, early), "rules_gather", [disp_shape, acc_shape],
        [*inputs(early), *weights, disp, acc], scratch(early), {k: 0, k + 1: 1},
    )
    shapes = [disp_shape, bf(late, width_f), bf(late, regions)]
    state, at = [disp], 0
    for ms in middle:
        k = len(ms) + 4
        state = call(
            functools.partial(middle_kernel, cfg, ms, at), "rules_middle", shapes,
            [*inputs(ms), *weights, *state], aliases={k + i: i for i in range(len(state))},
        )
        at += len(ms) * n
    k = len(last) + 5
    send, disp, feat, slope = call(
        functools.partial(last_kernel, cfg, last, at, row_scale), "rules_last",
        [bf(max(groups - 1, 1), regions, share), *shapes],
        [acc, *inputs(last), *weights, *state], aliases={k + i: 1 + i for i in range(len(state))},
    )
    decisions, grad = call(
        functools.partial(finish_kernel, groups, row_scale), "rules_finish",
        [bf(hour_blk, paths, regions), f32(regions, share)], [feat, slope, acc, disp],
    )
    for step in range(1, groups):
        pairs = [(g, (g + step) % groups) for g in range(groups)]
        grad = grad + lax.ppermute(send[step - 1], "grp", pairs).astype(F32)
    return decisions, grad.T[None]


def solution(mesh):
    return jax.shard_map(
        body,
        mesh=mesh,
        in_specs=(P(("grp", "blk"), None, None), P(), P(), P("blk", None, None), P("blk", None)),
        out_specs=(P("blk", "grp", None), P("blk", "grp", None)),
        check_vma=False,
    )
```

```python
import functools
import math

import jax
import jax.numpy as jnp
from jax import lax
from jax.experimental import pallas as pl
from jax.experimental.pallas import tpu as pltpu
from jax.sharding import PartitionSpec as P

F32 = jnp.float32
BF16 = jnp.bfloat16
LANES = 128
PLANE = 4


def dot(a, b, ca, cb):
    return lax.dot_general(a, b, (((ca,), (cb,)), ((), ())), preferred_element_type=F32)


def block_of(size, target):
    while size % target:
        target //= 2
    return target


def cuts_of(regions):
    return [(i, c, min(LANES, regions - c)) for i, c in enumerate(range(0, regions, LANES))]


def flips(groups, blocks):
    return groups % 2 == 0 and blocks == PLANE * PLANE


def digits(cfg):
    groups, blocks = cfg
    me = lax.axis_index("blk")
    hi, lo = me // PLANE, me % PLANE
    if not flips(groups, blocks):
        return hi, lo, None
    flip = lax.axis_index("grp") % 2
    return jnp.where(flip, lo, hi), jnp.where(flip, hi, lo), flip


def block_id(a, b, flip):
    straight = a * PLANE + b
    return straight if flip is None else jnp.where(flip, b * PLANE + a, straight)


FIRST_HOPS = (2, 1, 3)
SECOND_HOPS = (2, 1, 3)
FLIPPED_SECOND_HOPS = (1, 2, 3)


def first_distance(k, radix):
    if not k:
        return 0
    return FIRST_HOPS[k - 1] if radix == PLANE else radix - k


def second_distance(m, flip):
    if not m:
        return 0
    straight, flipped = SECOND_HOPS[m - 1], FLIPPED_SECOND_HOPS[m - 1]
    return straight if flip is None else jnp.where(flip, flipped, straight)


def pack_kernel(cfg, x_ref, *outs):
    a, _, flip = digits(cfg)
    for k, out in enumerate(outs):
        for b in range(PLANE):
            out[b] = x_ref[:, block_id(a ^ first_distance(k, len(outs)), b, flip)]


def front(x, weights, feat, slope, at):
    load_ref, net_ref, weight_ref, bias_ref = weights
    here = pl.ds(at, x.shape[0])
    width_f = load_ref.shape[1]
    step = block_of(width_f, 512)
    for c in range(0, width_f, step):
        y = jnp.dot(x, load_ref[:, pl.ds(c, step)], preferred_element_type=F32)
        feat[here, pl.ds(c, step)] = jnp.tanh(y).astype(BF16)
    net = dot(x, net_ref[...], 1, 1).astype(BF16).astype(F32)
    d = dot(feat[here, :], weight_ref[...], 1, 1) + bias_ref[...]
    slope[here, :] = (-1.5 - 2.5 * jnp.tanh(0.5 * (net - d)) + 0.25 * d).astype(BF16)
    return d


def rules(cfg, arrived, weights, disp_ref, feat, slope):
    a, b, flip = digits(cfg)
    radix = len(arrived[0][1])
    path_dev, hour_blk, width_k = arrived[0][1][0].shape
    piece = path_dev * hour_blk
    per = block_of(radix, max(256 // piece, 1))
    at = 0
    for m, parts in arrived:
        for k in range(0, radix, per):
            x = jnp.concatenate([p[...].reshape(piece, width_k) for p in parts[k : k + per]], 0)
            d = front(x, weights, feat, slope, at)
            for i in range(per):
                start = pl.multiple_of(block_id(a ^ first_distance(k + i, radix), b ^ second_distance(m, flip), flip) * piece, 16)
                for j, c, w in cuts_of(d.shape[1]):
                    disp_ref[j, pl.ds(start, piece), pl.ds(0, w)] = d[i * piece : (i + 1) * piece, c : c + w]
            at += per * piece


def grad_parts(groups, slope, feat, steps):
    share = feat.shape[1] // groups
    mine = lax.axis_index("grp")
    s = slope[...]
    width = block_of(share, 512)
    for step in steps:
        owner = lax.rem(mine + step, groups)
        for c in range(0, share, width):
            at = pl.ds(pl.multiple_of(owner * share + c, LANES), width)
            yield step - 1, pl.ds(c, width), dot(s, feat[:, at], 0, 0)


def load_kernel(*refs):
    k = len(refs) // 2
    for source, out in zip(refs[:k], refs[k:]):
        out[...] = source[...]


def own_digit(cfg, parts, weights, disp_ref, acc_ref, slope, feat):
    _, b, _ = digits(cfg)
    rules(cfg, [(0, [p.at[b] for p in parts])], weights, disp_ref, feat, slope)
    for i, at, g in grad_parts(cfg[0], slope, feat, range(1, cfg[0] + 1)):
        acc_ref[i, :, at] = g


def turn_kernel(cfg, radix, *refs):
    parts, weights, refs = refs[:radix], refs[radix : radix + 4], refs[radix + 4 :]
    outs, (disp_ref, acc_ref, slope, feat) = refs[:-4], refs[-4:]
    _, b, flip = digits(cfg)
    if flip is not None:
        @pl.when(flip == 1)
        def _():
            own_digit(cfg, parts, weights, disp_ref, acc_ref, slope, feat)
    for m, out in enumerate(outs, 1):
        for k, part in enumerate(parts):
            out[k] = part[b ^ second_distance(m, flip)]


def first_kernel(cfg, radix, *refs):
    parts, weights, refs = refs[:radix], refs[radix : radix + 4], refs[radix + 4 :]
    disp_in, acc_in, disp_ref, acc_ref, slope, feat = refs
    _, _, flip = digits(cfg)
    if flip is None:
        own_digit(cfg, parts, weights, disp_ref, acc_ref, slope, feat)
    else:
        @pl.when(flip == 0)
        def _():
            own_digit(cfg, parts, weights, disp_ref, acc_ref, slope, feat)


def gather_kernel(cfg, ms, *refs):
    k = len(ms)
    xs, weights, refs = refs[:k], refs[k : k + 4], refs[k + 4 :]
    disp_in, acc_in, disp_ref, acc_ref, slope, feat = refs
    rules(cfg, [(m, [x.at[i] for i in range(x.shape[0])]) for m, x in zip(ms, xs)], weights, disp_ref, feat, slope)
    for i, cols, g in grad_parts(cfg[0], slope, feat, range(1, cfg[0] + 1)):
        acc_ref[i, :, cols] = g + acc_in[i, :, cols]


def middle_kernel(cfg, ms, at, *refs):
    k = len(ms)
    xs, weights, refs = refs[:k], refs[k : k + 4], refs[k + 4 :]
    disp_ref, feat, slope = refs[-3:]
    rows = sum(math.prod(x.shape[:-1]) for x in xs)
    here = pl.ds(at, rows)
    rules(
        cfg, [(m, [x.at[i] for i in range(x.shape[0])]) for m, x in zip(ms, xs)], weights, disp_ref,
        feat.at[here], slope.at[here],
    )


def last_kernel(cfg, ms, at, row_scale, *refs):
    acc_ref, send_ref, refs = refs[0], refs[-4], refs[1:-4] + refs[-3:]
    middle_kernel(cfg, ms, at, *refs)
    _, feat, slope = refs[-3:]
    for i, cols, g in grad_parts(cfg[0], slope, feat, range(1, cfg[0])):
        send_ref[i, :, cols] = ((g + acc_ref[i, :, cols]) * row_scale).astype(BF16)


def finish_kernel(groups, row_scale, feat, slope, acc_ref, disp_ref, dec_ref, own_ref):
    hour_blk, paths, regions = dec_ref.shape
    for i, cols, g in grad_parts(groups, slope, feat, [groups]):
        own_ref[:, cols] = (g + acc_ref[i, :, cols]) * row_scale
    for h in range(hour_blk):
        for i, c, w in cuts_of(regions):
            dec_ref[h, :, pl.ds(c, w)] = disp_ref[i, pl.ds(h, paths, stride=hour_blk), :][:, :w].astype(BF16)


def call(kernel, name, outs, operands, scratch=(), aliases=None):
    vmem = pl.BlockSpec(memory_space=pltpu.VMEM)
    return pl.pallas_call(
        kernel,
        out_shape=tuple(outs),
        in_specs=[vmem] * len(operands),
        out_specs=[vmem] * len(outs),
        scratch_shapes=list(scratch),
        input_output_aliases=aliases or {},
        compiler_params=pltpu.CompilerParams(vmem_limit_bytes=16 << 20),
        cost_estimate=pl.CostEstimate(flops=0, bytes_accessed=0, transcendentals=0),
        name=name,
    )(*operands)


def body(factors, loadings, netload_map, rule_weights, rule_bias):
    blocks = lax.axis_size("blk")
    groups = lax.axis_size("grp")
    path_dev, hours, width_k = factors.shape
    width_f = loadings.shape[1]
    regions = netload_map.shape[1]
    hour_blk = hours // blocks
    paths = path_dev * blocks
    rows = paths * hour_blk
    share = width_f // groups
    radix = blocks // PLANE
    row_scale = 1.0 / math.sqrt(groups * rows)
    cfg = (groups, blocks)

    def bf(*shape):
        return jax.ShapeDtypeStruct(shape, BF16)

    def f32(*shape):
        return jax.ShapeDtypeStruct(shape, F32)

    def hop(x, straight, flipped):
        pairs = []
        for g in range(groups):
            distance = flipped if flips(groups, blocks) and g % 2 else straight
            pairs += [(g * blocks + i, g * blocks + (i ^ distance)) for i in range(blocks)]
        return lax.ppermute(x, ("grp", "blk"), pairs)

    parts = call(
        functools.partial(pack_kernel, cfg), "pack",
        [bf(PLANE, path_dev, hour_blk, width_k)] * radix,
        [factors.reshape(path_dev, blocks, hour_blk, width_k)],
    )
    dist = [first_distance(k, radix) for k in range(radix)]
    parts = [hop(x, d * PLANE, d) if d else x for d, x in zip(dist, parts)]
    weights = (loadings, netload_map.T, rule_weights[0].T, rule_bias)
    weights = call(
        load_kernel, "load", [jax.ShapeDtypeStruct(w.shape, w.dtype) for w in weights], weights,
    )
    disp_shape = f32(pl.cdiv(regions, LANES), rows, LANES)
    acc_shape = f32(groups, regions, share)

    def scratch(ms):
        n = len(ms) * rows // PLANE
        return [pltpu.VMEM((n, regions), BF16), pltpu.VMEM((n, width_f), BF16)]

    def inputs(ms):
        return [arrived[m] for m in ms]

    middle, last = [[1], [2]], [3]
    *turned, disp, acc = call(
        functools.partial(turn_kernel, cfg, radix), "turn",
        [bf(radix, path_dev, hour_blk, width_k)] * (PLANE - 1) + [disp_shape, acc_shape],
        [*parts, *weights], scratch([0]),
    )
    arrived = {m: hop(x, SECOND_HOPS[m - 1], FLIPPED_SECOND_HOPS[m - 1] * PLANE) for m, x in enumerate(turned, 1)}
    k = radix + 4
    disp, acc = call(
        functools.partial(first_kernel, cfg, radix), "rules_first",
        [disp_shape, acc_shape], [*parts, *weights, disp, acc], scratch([0]), {k: 0, k + 1: 1},
    )
    n = rows // PLANE
    early, middle = middle[0], middle[1:]
    late = (PLANE - 1 - len(early)) * n
    k = len(early) + 4
    disp, acc = call(
        functools.partial(gather_kernel, cfg, early), "rules_gather", [disp_shape, acc_shape],
        [*inputs(early), *weights, disp, acc], scratch(early), {k: 0, k + 1: 1},
    )
    shapes = [disp_shape, bf(late, width_f), bf(late, regions)]
    state, at = [disp], 0
    for ms in middle:
        k = len(ms) + 4
        state = call(
            functools.partial(middle_kernel, cfg, ms, at), "rules_middle", shapes,
            [*inputs(ms), *weights, *state], aliases={k + i: i for i in range(len(state))},
        )
        at += len(ms) * n
    k = len(last) + 5
    send, disp, feat, slope = call(
        functools.partial(last_kernel, cfg, last, at, row_scale), "rules_last",
        [bf(max(groups - 1, 1), regions, share), *shapes],
        [acc, *inputs(last), *weights, *state], aliases={k + i: 1 + i for i in range(len(state))},
    )
    decisions, grad = call(
        functools.partial(finish_kernel, groups, row_scale), "rules_finish",
        [bf(hour_blk, paths, regions), f32(regions, share)], [feat, slope, acc, disp],
    )
    for step in range(1, groups):
        pairs = [(g, (g + step) % groups) for g in range(groups)]
        grad = grad + lax.ppermute(send[step - 1], "grp", pairs).astype(F32)
    return decisions, grad.T[None]


def solution(mesh):
    return jax.shard_map(
        body,
        mesh=mesh,
        in_specs=(P(("grp", "blk"), None, None), P(), P(), P("blk", None, None), P("blk", None)),
        out_specs=(P("blk", "grp", None), P("blk", "grp", None)),
        check_vma=False,
    )
```

```python
import functools
import math

import jax
import jax.numpy as jnp
from jax import lax
from jax.experimental import pallas as pl
from jax.experimental.pallas import tpu as pltpu
from jax.sharding import PartitionSpec as P

F32 = jnp.float32
BF16 = jnp.bfloat16
LANES = 128
PLANE = 4


def dot(a, b, ca, cb):
    return lax.dot_general(a, b, (((ca,), (cb,)), ((), ())), preferred_element_type=F32)


def block_of(size, target):
    while size % target:
        target //= 2
    return target


def cuts_of(regions):
    return [(i, c, min(LANES, regions - c)) for i, c in enumerate(range(0, regions, LANES))]


def flips(groups, blocks):
    return groups % 2 == 0 and blocks == PLANE * PLANE


def digits(cfg):
    groups, blocks = cfg
    me = lax.axis_index("blk")
    hi, lo = me // PLANE, me % PLANE
    if not flips(groups, blocks):
        return hi, lo, None
    flip = lax.axis_index("grp") % 2
    return jnp.where(flip, lo, hi), jnp.where(flip, hi, lo), flip


def block_id(a, b, flip):
    straight = a * PLANE + b
    return straight if flip is None else jnp.where(flip, b * PLANE + a, straight)


FIRST_HOPS = (2, 1, 3)
SECOND_HOPS = (2, 1, 3)
FLIPPED_SECOND_HOPS = (1, 2, 3)


def first_distance(k, radix):
    if not k:
        return 0
    return FIRST_HOPS[k - 1] if radix == PLANE else radix - k


def second_distance(m, flip):
    if not m:
        return 0
    straight, flipped = SECOND_HOPS[m - 1], FLIPPED_SECOND_HOPS[m - 1]
    return straight if flip is None else jnp.where(flip, flipped, straight)


def pack_kernel(cfg, x_ref, *outs):
    a, _, flip = digits(cfg)
    for k, out in enumerate(outs):
        for b in range(PLANE):
            out[b] = x_ref[:, block_id(a ^ first_distance(k, len(outs)), b, flip)]


def front(x, weights, feat, slope, at):
    load_ref, net_ref, weight_ref, bias_ref = weights
    here = pl.ds(at, x.shape[0])
    width_f = load_ref.shape[1]
    step = block_of(width_f, 512)
    for c in range(0, width_f, step):
        y = jnp.dot(x, load_ref[:, pl.ds(c, step)], preferred_element_type=F32)
        feat[here, pl.ds(c, step)] = jnp.tanh(y).astype(BF16)
    net = dot(x, net_ref[...], 1, 1).astype(BF16).astype(F32)
    d = dot(feat[here, :], weight_ref[...], 1, 1) + bias_ref[...]
    slope[here, :] = (-1.5 - 2.5 * jnp.tanh(0.5 * (net - d)) + 0.25 * d).astype(BF16)
    return d


def rules(cfg, arrived, weights, disp_ref, feat, slope):
    a, b, flip = digits(cfg)
    radix = len(arrived[0][1])
    path_dev, hour_blk, width_k = arrived[0][1][0].shape
    piece = path_dev * hour_blk
    per = block_of(radix, max(256 // piece, 1))
    at = 0
    for m, parts in arrived:
        for k in range(0, radix, per):
            x = jnp.concatenate([p[...].reshape(piece, width_k) for p in parts[k : k + per]], 0)
            d = front(x, weights, feat, slope, at)
            for i in range(per):
                start = pl.multiple_of(block_id(a ^ first_distance(k + i, radix), b ^ second_distance(m, flip), flip) * piece, 16)
                for j, c, w in cuts_of(d.shape[1]):
                    disp_ref[j, pl.ds(start, piece), pl.ds(0, w)] = d[i * piece : (i + 1) * piece, c : c + w]
            at += per * piece


def grad_parts(groups, slope, feat, steps):
    share = feat.shape[1] // groups
    mine = lax.axis_index("grp")
    s = slope[...]
    width = block_of(share, 512)
    for step in steps:
        owner = lax.rem(mine + step, groups)
        for c in range(0, share, width):
            at = pl.ds(pl.multiple_of(owner * share + c, LANES), width)
            yield step - 1, pl.ds(c, width), dot(s, feat[:, at], 0, 0)


def load_kernel(*refs):
    k = len(refs) // 2
    for source, out in zip(refs[:k], refs[k:]):
        out[...] = source[...]


def own_digit(cfg, parts, weights, disp_ref, acc_ref, slope, feat):
    _, b, _ = digits(cfg)
    rules(cfg, [(0, [p.at[b] for p in parts])], weights, disp_ref, feat, slope)
    for i, at, g in grad_parts(cfg[0], slope, feat, range(1, cfg[0] + 1)):
        acc_ref[i, :, at] = g


def turn_kernel(cfg, radix, *refs):
    parts, weights, refs = refs[:radix], refs[radix : radix + 4], refs[radix + 4 :]
    outs, (disp_ref, acc_ref, slope, feat) = refs[:-4], refs[-4:]
    _, b, flip = digits(cfg)
    if flip is not None:
        @pl.when(flip == 1)
        def _():
            own_digit(cfg, parts, weights, disp_ref, acc_ref, slope, feat)
    for m, out in enumerate(outs, 1):
        for k, part in enumerate(parts):
            out[k] = part[b ^ second_distance(m, flip)]


def first_kernel(cfg, radix, *refs):
    parts, weights, refs = refs[:radix], refs[radix : radix + 4], refs[radix + 4 :]
    disp_in, acc_in, disp_ref, acc_ref, slope, feat = refs
    _, _, flip = digits(cfg)
    if flip is None:
        own_digit(cfg, parts, weights, disp_ref, acc_ref, slope, feat)
    else:
        @pl.when(flip == 0)
        def _():
            own_digit(cfg, parts, weights, disp_ref, acc_ref, slope, feat)


def gather_kernel(cfg, ms, *refs):
    k = len(ms)
    xs, weights, refs = refs[:k], refs[k : k + 4], refs[k + 4 :]
    disp_in, acc_in, disp_ref, acc_ref, slope, feat = refs
    rules(cfg, [(m, [x.at[i] for i in range(x.shape[0])]) for m, x in zip(ms, xs)], weights, disp_ref, feat, slope)
    for i, cols, g in grad_parts(cfg[0], slope, feat, range(1, cfg[0] + 1)):
        acc_ref[i, :, cols] = g + acc_in[i, :, cols]


def middle_kernel(cfg, ms, at, *refs):
    k = len(ms)
    xs, weights, refs = refs[:k], refs[k : k + 4], refs[k + 4 :]
    disp_ref, feat, slope = refs[-3:]
    rows = sum(math.prod(x.shape[:-1]) for x in xs)
    here = pl.ds(at, rows)
    rules(
        cfg, [(m, [x.at[i] for i in range(x.shape[0])]) for m, x in zip(ms, xs)], weights, disp_ref,
        feat.at[here], slope.at[here],
    )


def last_kernel(cfg, ms, at, row_scale, *refs):
    acc_ref, send_ref, refs = refs[0], refs[-4], refs[1:-4] + refs[-3:]
    middle_kernel(cfg, ms, at, *refs)
    _, feat, slope = refs[-3:]
    for i, cols, g in grad_parts(cfg[0], slope, feat, range(1, cfg[0])):
        send_ref[i, :, cols] = ((g + acc_ref[i, :, cols]) * row_scale).astype(BF16)


def finish_kernel(groups, row_scale, feat, slope, acc_ref, disp_ref, dec_ref, own_ref):
    hour_blk, paths, regions = dec_ref.shape
    for i, cols, g in grad_parts(groups, slope, feat, [groups]):
        own_ref[:, cols] = (g + acc_ref[i, :, cols]) * row_scale
    for h in range(hour_blk):
        for i, c, w in cuts_of(regions):
            dec_ref[h, :, pl.ds(c, w)] = disp_ref[i, pl.ds(h, paths, stride=hour_blk), :][:, :w].astype(BF16)


def add_kernel(own_ref, *refs):
    received, out, stage, sem = refs[:-3], refs[-3], refs[-2], refs[-1]
    n = sem.shape[0]
    width = own_ref.shape[1] // n
    copies = []
    for i in range(n):
        cols = pl.ds(i * width, width)
        total = own_ref[:, cols]
        for r in received:
            total = total + r[:, cols].astype(F32)
        stage[:, cols] = total
        copies.append(pltpu.make_async_copy(stage.at[:, cols], out.at[:, cols], sem.at[i]))
        copies[-1].start()
    for c in copies:
        c.wait()


def call(kernel, name, outs, operands, scratch=(), aliases=None):
    vmem = pl.BlockSpec(memory_space=pltpu.VMEM)
    return pl.pallas_call(
        kernel,
        out_shape=tuple(outs),
        in_specs=[vmem] * len(operands),
        out_specs=[vmem] * len(outs),
        scratch_shapes=list(scratch),
        input_output_aliases=aliases or {},
        compiler_params=pltpu.CompilerParams(vmem_limit_bytes=16 << 20),
        cost_estimate=pl.CostEstimate(flops=0, bytes_accessed=0, transcendentals=0),
        name=name,
    )(*operands)


def body(factors, loadings, netload_map, rule_weights, rule_bias):
    blocks = lax.axis_size("blk")
    groups = lax.axis_size("grp")
    path_dev, hours, width_k = factors.shape
    width_f = loadings.shape[1]
    regions = netload_map.shape[1]
    hour_blk = hours // blocks
    paths = path_dev * blocks
    rows = paths * hour_blk
    share = width_f // groups
    radix = blocks // PLANE
    row_scale = 1.0 / math.sqrt(groups * rows)
    cfg = (groups, blocks)

    def bf(*shape):
        return jax.ShapeDtypeStruct(shape, BF16)

    def f32(*shape):
        return jax.ShapeDtypeStruct(shape, F32)

    def hop(x, straight, flipped):
        pairs = []
        for g in range(groups):
            distance = flipped if flips(groups, blocks) and g % 2 else straight
            pairs += [(g * blocks + i, g * blocks + (i ^ distance)) for i in range(blocks)]
        return lax.ppermute(x, ("grp", "blk"), pairs)

    parts = call(
        functools.partial(pack_kernel, cfg), "pack",
        [bf(PLANE, path_dev, hour_blk, width_k)] * radix,
        [factors.reshape(path_dev, blocks, hour_blk, width_k)],
    )
    dist = [first_distance(k, radix) for k in range(radix)]
    parts = [hop(x, d * PLANE, d) if d else x for d, x in zip(dist, parts)]
    weights = (loadings, netload_map.T, rule_weights[0].T, rule_bias)
    weights = call(
        load_kernel, "load", [jax.ShapeDtypeStruct(w.shape, w.dtype) for w in weights], weights,
    )
    disp_shape = f32(pl.cdiv(regions, LANES), rows, LANES)
    acc_shape = f32(groups, regions, share)

    def scratch(ms):
        n = len(ms) * rows // PLANE
        return [pltpu.VMEM((n, regions), BF16), pltpu.VMEM((n, width_f), BF16)]

    def inputs(ms):
        return [arrived[m] for m in ms]

    middle, last = [[1], [2]], [3]
    *turned, disp, acc = call(
        functools.partial(turn_kernel, cfg, radix), "turn",
        [bf(radix, path_dev, hour_blk, width_k)] * (PLANE - 1) + [disp_shape, acc_shape],
        [*parts, *weights], scratch([0]),
    )
    arrived = {m: hop(x, SECOND_HOPS[m - 1], FLIPPED_SECOND_HOPS[m - 1] * PLANE) for m, x in enumerate(turned, 1)}
    k = radix + 4
    disp, acc = call(
        functools.partial(first_kernel, cfg, radix), "rules_first",
        [disp_shape, acc_shape], [*parts, *weights, disp, acc], scratch([0]), {k: 0, k + 1: 1},
    )
    n = rows // PLANE
    early, middle = middle[0], middle[1:]
    late = (PLANE - 1 - len(early)) * n
    k = len(early) + 4
    disp, acc = call(
        functools.partial(gather_kernel, cfg, early), "rules_gather", [disp_shape, acc_shape],
        [*inputs(early), *weights, disp, acc], scratch(early), {k: 0, k + 1: 1},
    )
    shapes = [disp_shape, bf(late, width_f), bf(late, regions)]
    state, at = [disp], 0
    for ms in middle:
        k = len(ms) + 4
        state = call(
            functools.partial(middle_kernel, cfg, ms, at), "rules_middle", shapes,
            [*inputs(ms), *weights, *state], aliases={k + i: i for i in range(len(state))},
        )
        at += len(ms) * n
    k = len(last) + 5
    send, disp, feat, slope = call(
        functools.partial(last_kernel, cfg, last, at, row_scale), "rules_last",
        [bf(max(groups - 1, 1), regions, share), *shapes],
        [acc, *inputs(last), *weights, *state], aliases={k + i: 1 + i for i in range(len(state))},
    )
    decisions, grad = call(
        functools.partial(finish_kernel, groups, row_scale), "rules_finish",
        [bf(hour_blk, paths, regions), f32(regions, share)], [feat, slope, acc, disp],
    )
    received = []
    for step in range(1, groups):
        pairs = [(g, (g + step) % groups) for g in range(groups)]
        received.append(lax.ppermute(send[step - 1], "grp", pairs))
    vmem, hbm = pl.BlockSpec(memory_space=pltpu.VMEM), pl.BlockSpec(memory_space=pl.ANY)
    chunks = block_of(share // LANES, 4)
    grad = pl.pallas_call(
        add_kernel, out_shape=f32(regions, share), in_specs=[vmem] * groups, out_specs=hbm,
        scratch_shapes=[pltpu.VMEM((regions, share), F32), pltpu.SemaphoreType.DMA((chunks,))],
        compiler_params=pltpu.CompilerParams(vmem_limit_bytes=16 << 20), name="add",
    )(grad, *received)
    return decisions, grad.T[None]


def solution(mesh):
    return jax.shard_map(
        body,
        mesh=mesh,
        in_specs=(P(("grp", "blk"), None, None), P(), P(), P("blk", None, None), P("blk", None)),
        out_specs=(P("blk", "grp", None), P("blk", "grp", None)),
        check_vma=False,
    )
```

```python
import functools
import math

import jax
import jax.numpy as jnp
from jax import lax
from jax.experimental import pallas as pl
from jax.experimental.pallas import tpu as pltpu
from jax.sharding import PartitionSpec as P

F32 = jnp.float32
BF16 = jnp.bfloat16
LANES = 128
PLANE = 4


def dot(a, b, ca, cb):
    return lax.dot_general(a, b, (((ca,), (cb,)), ((), ())), preferred_element_type=F32)


def block_of(size, target):
    while size % target:
        target //= 2
    return target


def cuts_of(regions):
    return [(i, c, min(LANES, regions - c)) for i, c in enumerate(range(0, regions, LANES))]


def flips(groups, blocks):
    return groups % 2 == 0 and blocks == PLANE * PLANE


def digits(cfg):
    groups, blocks = cfg
    me = lax.axis_index("blk")
    hi, lo = me // PLANE, me % PLANE
    if not flips(groups, blocks):
        return hi, lo, None
    flip = lax.axis_index("grp") % 2
    return jnp.where(flip, lo, hi), jnp.where(flip, hi, lo), flip


def block_id(a, b, flip):
    straight = a * PLANE + b
    return straight if flip is None else jnp.where(flip, b * PLANE + a, straight)


FIRST_HOPS = (2, 1, 3)
SECOND_HOPS = (2, 1, 3)
FLIPPED_SECOND_HOPS = (1, 2, 3)


def first_distance(k, radix):
    if not k:
        return 0
    return FIRST_HOPS[k - 1] if radix == PLANE else radix - k


def second_distance(m, flip):
    if not m:
        return 0
    straight, flipped = SECOND_HOPS[m - 1], FLIPPED_SECOND_HOPS[m - 1]
    return straight if flip is None else jnp.where(flip, flipped, straight)


def pack_kernel(cfg, x_ref, *outs):
    a, _, flip = digits(cfg)
    for k, out in enumerate(outs):
        for b in range(PLANE):
            out[b] = x_ref[:, block_id(a ^ first_distance(k, len(outs)), b, flip)]


def front(x, weights, feat, slope, at):
    load_ref, net_ref, weight_ref, bias_ref = weights
    here = pl.ds(at, x.shape[0])
    width_f = load_ref.shape[1]
    step = block_of(width_f, 512)
    for c in range(0, width_f, step):
        y = jnp.dot(x, load_ref[:, pl.ds(c, step)], preferred_element_type=F32)
        feat[here, pl.ds(c, step)] = jnp.tanh(y).astype(BF16)
    net = dot(x, net_ref[...], 1, 1).astype(BF16).astype(F32)
    d = dot(feat[here, :], weight_ref[...], 1, 1) + bias_ref[...]
    slope[here, :] = (-1.5 - 2.5 * jnp.tanh(0.5 * (net - d)) + 0.25 * d).astype(BF16)
    return d


def rules(cfg, arrived, weights, disp_ref, feat, slope):
    a, b, flip = digits(cfg)
    radix = len(arrived[0][1])
    path_dev, hour_blk, width_k = arrived[0][1][0].shape
    piece = path_dev * hour_blk
    per = block_of(radix, max(256 // piece, 1))
    at = 0
    for m, parts in arrived:
        for k in range(0, radix, per):
            x = jnp.concatenate([p[...].reshape(piece, width_k) for p in parts[k : k + per]], 0)
            d = front(x, weights, feat, slope, at)
            for i in range(per):
                start = pl.multiple_of(block_id(a ^ first_distance(k + i, radix), b ^ second_distance(m, flip), flip) * piece, 16)
                for j, c, w in cuts_of(d.shape[1]):
                    disp_ref[j, pl.ds(start, piece), pl.ds(0, w)] = d[i * piece : (i + 1) * piece, c : c + w]
            at += per * piece


def grad_parts(groups, slope, feat, steps):
    share = feat.shape[1] // groups
    mine = lax.axis_index("grp")
    s = slope[...]
    width = block_of(share, 512)
    for step in steps:
        owner = lax.rem(mine + step, groups)
        for c in range(0, share, width):
            at = pl.ds(pl.multiple_of(owner * share + c, LANES), width)
            yield step - 1, pl.ds(c, width), dot(s, feat[:, at], 0, 0)


def load_kernel(*refs):
    k = len(refs) // 2
    for source, out in zip(refs[:k], refs[k:]):
        out[...] = source[...]


def own_digit(cfg, parts, weights, disp_ref, acc_ref, slope, feat):
    _, b, _ = digits(cfg)
    rules(cfg, [(0, [p.at[b] for p in parts])], weights, disp_ref, feat, slope)
    for i, at, g in grad_parts(cfg[0], slope, feat, range(1, cfg[0] + 1)):
        acc_ref[i, :, at] = g


def turn_kernel(cfg, radix, *refs):
    parts, weights, refs = refs[:radix], refs[radix : radix + 4], refs[radix + 4 :]
    outs, (disp_ref, acc_ref, slope, feat) = refs[:-4], refs[-4:]
    _, b, flip = digits(cfg)
    if flip is not None:
        @pl.when(flip == 1)
        def _():
            own_digit(cfg, parts, weights, disp_ref, acc_ref, slope, feat)
    for m, out in enumerate(outs, 1):
        for k, part in enumerate(parts):
            out[k] = part[b ^ second_distance(m, flip)]


def first_kernel(cfg, radix, *refs):
    parts, weights, refs = refs[:radix], refs[radix : radix + 4], refs[radix + 4 :]
    disp_in, acc_in, disp_ref, acc_ref, slope, feat = refs
    _, _, flip = digits(cfg)
    if flip is None:
        own_digit(cfg, parts, weights, disp_ref, acc_ref, slope, feat)
    else:
        @pl.when(flip == 0)
        def _():
            own_digit(cfg, parts, weights, disp_ref, acc_ref, slope, feat)


def gather_kernel(cfg, ms, *refs):
    k = len(ms)
    xs, weights, refs = refs[:k], refs[k : k + 4], refs[k + 4 :]
    disp_in, acc_in, disp_ref, acc_ref, slope, feat = refs
    rules(cfg, [(m, [x.at[i] for i in range(x.shape[0])]) for m, x in zip(ms, xs)], weights, disp_ref, feat, slope)
    for i, cols, g in grad_parts(cfg[0], slope, feat, range(1, cfg[0] + 1)):
        acc_ref[i, :, cols] = g + acc_in[i, :, cols]


def middle_kernel(cfg, ms, at, *refs):
    k = len(ms)
    xs, weights, refs = refs[:k], refs[k : k + 4], refs[k + 4 :]
    disp_ref, feat, slope = refs[-3:]
    rows = sum(math.prod(x.shape[:-1]) for x in xs)
    here = pl.ds(at, rows)
    rules(
        cfg, [(m, [x.at[i] for i in range(x.shape[0])]) for m, x in zip(ms, xs)], weights, disp_ref,
        feat.at[here], slope.at[here],
    )


def last_kernel(cfg, ms, at, row_scale, *refs):
    acc_ref, send_ref, part, refs = refs[0], refs[-5], refs[-1], refs[1:-5] + refs[-4:-1]
    _, feat, slope = refs[-3:]
    old, new = pl.ds(0, at), pl.ds(at, feat.shape[0] - at)
    for i, cols, g in grad_parts(cfg[0], slope.at[old], feat.at[old], range(1, cfg[0])):
        part[i, :, cols] = g + acc_ref[i, :, cols]
    middle_kernel(cfg, ms, at, *refs)
    for i, cols, g in grad_parts(cfg[0], slope.at[new], feat.at[new], range(1, cfg[0])):
        send_ref[i, :, cols] = ((g + part[i, :, cols]) * row_scale).astype(BF16)


def finish_kernel(groups, row_scale, feat, slope, acc_ref, disp_ref, dec_ref, own_ref):
    hour_blk, paths, regions = dec_ref.shape
    for i, cols, g in grad_parts(groups, slope, feat, [groups]):
        own_ref[:, cols] = (g + acc_ref[i, :, cols]) * row_scale
    for h in range(hour_blk):
        for i, c, w in cuts_of(regions):
            dec_ref[h, :, pl.ds(c, w)] = disp_ref[i, pl.ds(h, paths, stride=hour_blk), :][:, :w].astype(BF16)


def call(kernel, name, outs, operands, scratch=(), aliases=None):
    vmem = pl.BlockSpec(memory_space=pltpu.VMEM)
    return pl.pallas_call(
        kernel,
        out_shape=tuple(outs),
        in_specs=[vmem] * len(operands),
        out_specs=[vmem] * len(outs),
        scratch_shapes=list(scratch),
        input_output_aliases=aliases or {},
        compiler_params=pltpu.CompilerParams(vmem_limit_bytes=16 << 20),
        cost_estimate=pl.CostEstimate(flops=0, bytes_accessed=0, transcendentals=0),
        name=name,
    )(*operands)


def body(factors, loadings, netload_map, rule_weights, rule_bias):
    blocks = lax.axis_size("blk")
    groups = lax.axis_size("grp")
    path_dev, hours, width_k = factors.shape
    width_f = loadings.shape[1]
    regions = netload_map.shape[1]
    hour_blk = hours // blocks
    paths = path_dev * blocks
    rows = paths * hour_blk
    share = width_f // groups
    radix = blocks // PLANE
    row_scale = 1.0 / math.sqrt(groups * rows)
    cfg = (groups, blocks)

    def bf(*shape):
        return jax.ShapeDtypeStruct(shape, BF16)

    def f32(*shape):
        return jax.ShapeDtypeStruct(shape, F32)

    def hop(x, straight, flipped):
        pairs = []
        for g in range(groups):
            distance = flipped if flips(groups, blocks) and g % 2 else straight
            pairs += [(g * blocks + i, g * blocks + (i ^ distance)) for i in range(blocks)]
        return lax.ppermute(x, ("grp", "blk"), pairs)

    parts = call(
        functools.partial(pack_kernel, cfg), "pack",
        [bf(PLANE, path_dev, hour_blk, width_k)] * radix,
        [factors.reshape(path_dev, blocks, hour_blk, width_k)],
    )
    dist = [first_distance(k, radix) for k in range(radix)]
    parts = [hop(x, d * PLANE, d) if d else x for d, x in zip(dist, parts)]
    weights = (loadings, netload_map.T, rule_weights[0].T, rule_bias)
    weights = call(
        load_kernel, "load", [jax.ShapeDtypeStruct(w.shape, w.dtype) for w in weights], weights,
    )
    disp_shape = f32(pl.cdiv(regions, LANES), rows, LANES)
    acc_shape = f32(groups, regions, share)

    def scratch(ms):
        n = len(ms) * rows // PLANE
        return [pltpu.VMEM((n, regions), BF16), pltpu.VMEM((n, width_f), BF16)]

    def inputs(ms):
        return [arrived[m] for m in ms]

    middle, last = [[1], [2]], [3]
    *turned, disp, acc = call(
        functools.partial(turn_kernel, cfg, radix), "turn",
        [bf(radix, path_dev, hour_blk, width_k)] * (PLANE - 1) + [disp_shape, acc_shape],
        [*parts, *weights], scratch([0]),
    )
    arrived = {m: hop(x, SECOND_HOPS[m - 1], FLIPPED_SECOND_HOPS[m - 1] * PLANE) for m, x in enumerate(turned, 1)}
    k = radix + 4
    disp, acc = call(
        functools.partial(first_kernel, cfg, radix), "rules_first",
        [disp_shape, acc_shape], [*parts, *weights, disp, acc], scratch([0]), {k: 0, k + 1: 1},
    )
    n = rows // PLANE
    early, middle = middle[0], middle[1:]
    late = (PLANE - 1 - len(early)) * n
    k = len(early) + 4
    disp, acc = call(
        functools.partial(gather_kernel, cfg, early), "rules_gather", [disp_shape, acc_shape],
        [*inputs(early), *weights, disp, acc], scratch(early), {k: 0, k + 1: 1},
    )
    shapes = [disp_shape, bf(late, width_f), bf(late, regions)]
    state, at = [disp], 0
    for ms in middle:
        k = len(ms) + 4
        state = call(
            functools.partial(middle_kernel, cfg, ms, at), "rules_middle", shapes,
            [*inputs(ms), *weights, *state], aliases={k + i: i for i in range(len(state))},
        )
        at += len(ms) * n
    k = len(last) + 5
    send, disp, feat, slope = call(
        functools.partial(last_kernel, cfg, last, at, row_scale), "rules_last",
        [bf(max(groups - 1, 1), regions, share), *shapes],
        [acc, *inputs(last), *weights, *state],
        [pltpu.VMEM((max(groups - 1, 1), regions, share), F32)], {k + i: 1 + i for i in range(len(state))},
    )
    decisions, grad = call(
        functools.partial(finish_kernel, groups, row_scale), "rules_finish",
        [bf(hour_blk, paths, regions), f32(regions, share)], [feat, slope, acc, disp],
    )
    for step in range(1, groups):
        pairs = [(g, (g + step) % groups) for g in range(groups)]
        grad = grad + lax.ppermute(send[step - 1], "grp", pairs).astype(F32)
    return decisions, grad.T[None]


def solution(mesh):
    return jax.shard_map(
        body,
        mesh=mesh,
        in_specs=(P(("grp", "blk"), None, None), P(), P(), P("blk", None, None), P("blk", None)),
        out_specs=(P("blk", "grp", None), P("blk", "grp", None)),
        check_vma=False,
    )
```
